32 devices in a mesh: groups: 2 (over y), pts: 4 (over z), seg: 4 (over x, core).
Axes of the slice: x: 2, y: 2, z: 4, core: 2. Of those that a mesh axis runs over, the one named last changes fastest.
Arguments:
- field_points: float32 [3, 8192], P(None, ('groups', 'pts', 'seg')), parts along dimension 1, may hold values from -6 to 6
- wake_nodes: float32 [3, 65536], P(None, ('groups', 'seg')), parts along dimension 1, may hold values from -6 to 6
- trail_node: int32 [65536], P(('groups', 'seg')), parts along dimension 0, may hold values from 0 to 8191
- strength: float32 [65536], P(('groups', 'seg')), parts along dimension 0, may hold values from -3 to 3
- core_square: float32 [65536], P(('groups', 'seg')), parts along dimension 0, may hold values from 0.05 to 0.5
- snapshot: int32 [65536], P(('groups', 'seg')), parts along dimension 0, may hold values from 0 to 15
- stored_modes: float32 [512, 8192], P(None, ('groups', 'pts', 'seg')), parts along dimension 1, may hold values from -0.03125 to 0.03125
Outputs:
- coeffs: float32 [1024, 48], P('groups'), parts along dimension 0
- factor: float32 [96, 48], P('groups'), parts along dimension 0
- basis: float32 [48, 8192], P(None, ('groups', 'pts', 'seg')), parts along dimension 1
The draws below stay inside these ranges and needn't reach their ends.
There are 2 independent parts, one for each index of `groups`. The reference program is written for one: setup_inputs(seed, part) draws one part's arguments, and reference() takes and returns one part's arrays. A program takes and returns all parts, laid end to end along the dimension named above; each array names one. Nothing has to cross between parts.
All inputs are finite; a program needn't handle non-finite values.
Results may differ from the reference program's by a relative error of at most 0.0003.
Values sent between devices are 32-bit elements; how exact they have to be, the bound alone decides.
A program may use at most 192 MiB of HBM per device.

```python
import math
import jax
import jax.numpy as jnp
from jax import lax

SNAPS = 16
MODES = 512
SEGS = 32768
SEG_DEV = 8192
NP = 4096


def mode_rows(key, low_scale, high_scale, share):
    keys = jax.random.split(key, 4)
    noise = jnp.clip(jax.random.normal(keys[0], (MODES, NP), jnp.float32), -4.0, 4.0)
    common = jnp.clip(jax.random.normal(keys[1], (NP,), jnp.float32), -4.0, 4.0)
    scales = jnp.exp(jax.random.uniform(keys[2], (MODES, 1), jnp.float32, math.log(low_scale), math.log(high_scale)))
    signs = jnp.where(jax.random.randint(keys[3], (MODES, 1), 0, 2) == 1, 1.0, -1.0).astype(jnp.float32)
    mixed = scales * (math.sqrt(1.0 - share * share) * noise + share * signs * common[None, :])
    return jnp.clip(mixed / math.sqrt(NP), -0.03125, 0.03125).astype(jnp.float32)


def draw_stored_modes(key, part):
    key = jax.random.fold_in(key, 7)
    return mode_rows(key, 0.3, 3.0, 0.2)


def set_ends(drawn, stream_key, low, high):
    place = [jax.random.randint(jax.random.fold_in(stream_key, axis), (), 0, length) for axis, length in enumerate(drawn.shape)]
    main_axis = drawn.shape.index(max(drawn.shape))
    beside = place[:main_axis] + [(place[main_axis] + 1) % drawn.shape[main_axis]] + place[main_axis + 1:]
    return drawn.at[tuple(place)].set(low).at[tuple(beside)].set(high)


def block_scale(key, shape, cuts, least, largest):
    loudness = 1.0
    for axis_at, parts in cuts:
        heights = jax.random.uniform(jax.random.fold_in(jax.random.fold_in(key, 6), axis_at), (parts,), jnp.float32, least / len(cuts), largest / len(cuts))
        loudness = loudness * jnp.repeat(jnp.exp(heights), shape[axis_at] // parts).reshape((-1,) + (1,) * (len(shape) - 1 - axis_at))
    return loudness


def gaussian(stream_key, shape, width, bound, pieces=(), held_as=jnp.bfloat16):
    drawn = width * jax.random.normal(stream_key, shape, jnp.float32)
    if pieces:
        drawn = drawn * block_scale(stream_key, shape, pieces, -0.22, 0.18)
    return jnp.clip(drawn, -bound, bound).astype(held_as)


def setup_inputs(seed: int = 0, part: int = 0) -> dict:
    key_of = jax.random.split(jax.random.key(seed), 8)
    part_splits = jax.random.split(jax.random.fold_in(key_of[7], part), 8)
    field_points = gaussian(part_splits[0], (3, NP), 1.0, 6.0, ((1, 16),), jnp.float32)
    wake_nodes = gaussian(part_splits[1], (3, SEGS), 1.0, 6.0, ((1, 4),), jnp.float32)
    trail_node = set_ends(jax.random.randint(part_splits[2], (SEGS,), 0, SEG_DEV), jax.random.fold_in(part_splits[2], 1), 0, SEG_DEV - 1).astype(jnp.int32)
    strength = gaussian(part_splits[3], (SEGS,), 0.5, 3.0, ((0, 4),), jnp.float32)
    core_square = jnp.clip(jnp.exp(math.log(0.5) - 2.3025851 * jax.random.uniform(part_splits[4], (SEGS,), jnp.float32) ** block_scale(part_splits[4], (SEGS,), ((0, 4),), -0.2, 0.2)), 0.05, 0.5)
    snapshot = set_ends(jax.random.randint(part_splits[5], (SEGS,), 0, SNAPS), jax.random.fold_in(part_splits[5], 1), 0, SNAPS - 1).astype(jnp.int32)
    stored_modes = draw_stored_modes(jax.random.fold_in(jax.random.fold_in(key_of[7], part), 71), part)
    return dict(field_points=field_points, wake_nodes=wake_nodes, trail_node=trail_node, strength=strength, core_square=core_square, snapshot=snapshot, stored_modes=stored_modes)


HIGH = lax.Precision.HIGHEST
inv_four_pi = 1.0 / (4.0 * math.pi)

def induced_block(points, geometry, labels):
    seg_tail = geometry[0:3]
    seg_head = geometry[3:6]
    near_arm = points[:, :, None] - seg_tail[:, None, :]
    far_arm = points[:, :, None] - seg_head[:, None, :]
    core_sq = geometry[7][None, :]
    near_len = jnp.sqrt(lax.optimization_barrier(jnp.sum(near_arm * near_arm, axis=0)) + core_sq)
    far_len = jnp.sqrt(lax.optimization_barrier(jnp.sum(far_arm * far_arm, axis=0)) + core_sq)
    along_dot = lax.optimization_barrier(jnp.sum(near_arm * far_arm, axis=0))
    factor = (near_len + far_len) / (near_len * far_len * (near_len * far_len + along_dot))
    curl_dir = jnp.stack([near_arm[1] * far_arm[2] - near_arm[2] * far_arm[1], near_arm[2] * far_arm[0] - near_arm[0] * far_arm[2], near_arm[0] * far_arm[1] - near_arm[1] * far_arm[0]]) * factor[None]
    levels = jnp.arange(SNAPS, dtype=jnp.float32)
    weights = (labels[:, None] == levels[None, :]).astype(jnp.float32) * (geometry[6] * inv_four_pi)[:, None]
    induced = jnp.einsum('cpn,ns->csp', curl_dir, weights, precision=HIGH)
    return induced.reshape(3 * SNAPS, points.shape[1])

def reference(field_points, wake_nodes, trail_node, strength, core_square, snapshot, stored_modes):
    owner = jnp.arange(SEGS, dtype=jnp.int32) // SEG_DEV * SEG_DEV
    seg_ends = wake_nodes[:, owner + trail_node.astype(jnp.int32)]
    geometry = jnp.concatenate([wake_nodes, seg_ends, strength[None], core_square[None], snapshot.astype(jnp.float32)[None]], axis=0)
    block_width = math.gcd(SEGS, 512)
    block_count = SEGS // block_width
    geo_blocks = geometry.reshape(9, block_count, block_width).transpose(1, 0, 2)

    def absorb(running, geo_piece):
        return (running + induced_block(field_points, geo_piece, geo_piece[8]), None)
    panel, unused = lax.scan(absorb, jnp.zeros((3 * SNAPS, NP), jnp.float32), geo_blocks)
    coeffs = jnp.dot(stored_modes.astype(jnp.float32), panel.T.astype(jnp.float32), precision=HIGH, preferred_element_type=jnp.float32)
    projected = panel - jnp.dot(coeffs.T.astype(jnp.float32), stored_modes.astype(jnp.float32), precision=HIGH, preferred_element_type=jnp.float32)
    gram = jnp.dot(projected.astype(jnp.float32), projected.T.astype(jnp.float32), precision=HIGH, preferred_element_type=jnp.float32) / NP
    lower = jnp.linalg.cholesky(gram)
    basis = lax.linalg.triangular_solve(lower, projected, left_side=True, lower=True)
    return (coeffs, lower.T, basis)
```

```python
import functools
import math

import jax
import jax.numpy as jnp
from jax import lax
from jax.experimental import pallas as pl
from jax.experimental.pallas import tpu as pltpu
from jax.sharding import PartitionSpec as P

SNAPS = 16
HIGH = lax.Precision.HIGHEST
MESH = pl.DeviceIdType.MESH
DEPTH = 32
CHUNK = 256
GROUP = 4
f32 = jnp.float32
bf16 = jnp.bfloat16


def split3(v):
    hi = v.astype(bf16).astype(f32)
    rest = v - hi
    mid = rest.astype(bf16).astype(f32)
    return hi, mid, (rest - mid).astype(bf16).astype(f32)


def left_rows(v):
    hi, mid, lo = split3(v)
    return [hi, hi, mid, hi, lo, mid]


def right_rows(v):
    hi, mid, lo = split3(v)
    return [hi, mid, hi, lo, hi, mid]


def prep_kernel(nodes_ref, trail_ref, strength_ref, core_ref, snap_ref,
                near_ref, far_ref, weight_ref, centre_ref, head_ref):
    segs = nodes_ref.shape[1]
    rows = segs // 128
    nodes = nodes_ref[...]
    centre = jnp.sum(nodes, axis=1, keepdims=True) * (1.0 / segs)
    centre_ref[...] = jnp.broadcast_to(centre, centre_ref.shape)

    tiles = rows // 8
    high = [trail_ref[8 * r:8 * r + 8, :] // 128 for r in range(tiles)]
    low = [trail_ref[8 * r:8 * r + 8, :] % 128 for r in range(tiles)]

    def look(h, found):
        cols = pl.ds(pl.multiple_of(h * 128, 128), 128)
        out = list(found)
        table = [jnp.broadcast_to(nodes_ref[k:k + 1, cols], (8, 128)) for k in range(3)]
        for r in range(tiles):
            here = high[r] == h
            for k in range(3):
                got = jnp.take_along_axis(table[k], low[r], axis=1, mode="promise_in_bounds")
                out[3 * r + k] = jnp.where(here, got, out[3 * r + k])
        return tuple(out)

    found = lax.fori_loop(0, rows, look, tuple(jnp.zeros((8, 128), f32) for _ in range(3 * tiles)))
    for r in range(tiles):
        for k in range(3):
            for i in range(8):
                at = (8 * r + i) * 128
                head_ref[k:k + 1, at:at + 128] = found[3 * r + k][i:i + 1, :]

    width = 1024
    zero = jnp.zeros((1, width), f32)
    levels = lax.broadcasted_iota(jnp.int32, (SNAPS, width), 0)

    def fill(b, carry):
        cols = pl.ds(pl.multiple_of(b * width, 128), width)
        t = [nodes_ref[k:k + 1, cols] - centre[k:k + 1, :] for k in range(3)]
        h = [head_ref[k:k + 1, cols] - centre[k:k + 1, :] for k in range(3)]
        core = core_ref[:, cols]
        d = [t[k] - h[k] for k in range(3)]
        q = 2.0 * core + (d[0] * d[0] + d[1] * d[1] + d[2] * d[2])
        g = 1.0 / q
        for ref, e in ((near_ref, t), (far_ref, h)):
            square = e[0] * e[0] + e[1] * e[1] + e[2] * e[2] + core
            parts = []
            for k in range(3):
                parts += left_rows(-2.0 * g * e[k])
            parts += left_rows(g) + list(split3(g * square))
            parts += [zero] * (DEPTH - len(parts))
            packed = jnp.concatenate(parts, axis=0)
            ref[pl.ds(pl.multiple_of(b * width, 128), width), :] = packed.T.astype(bf16)
        scale = strength_ref[:, cols] * (2.0 / (4.0 * math.pi)) * g * jnp.sqrt(g)
        v = d + [t[1] * h[2] - t[2] * h[1], t[2] * h[0] - t[0] * h[2], t[0] * h[1] - t[1] * h[0]]
        mine = snap_ref[:, cols] == levels
        for k in range(6):
            value = v[k] * scale
            hi = value.astype(bf16).astype(f32)
            lo = value - hi
            at = SNAPS * k
            weight_ref[at:at + SNAPS, cols] = jnp.where(mine, hi, 0.0).astype(bf16)
            weight_ref[6 * SNAPS + at:6 * SNAPS + at + SNAPS, cols] = jnp.where(mine, lo, 0.0).astype(bf16)
        return carry

    lax.fori_loop(0, segs // width, fill, 0)


def main_kernel(pts_size, seg_size, points_ref, near_ref, far_ref, weight_ref, centre_ref, modes_ref,
                coeff_ref, gram_ref, proj_ref,
                peer_points, part_out, part_in, both_acc, low_acc, side, hi_buf, lo_buf,
                coeff_in, gram_in,
                point_send, point_recv, part_send, part_recv, coeff_send, coeff_recv, gram_send, gram_recv):
    group = lax.axis_index("groups")
    pts = lax.axis_index("pts")
    seg = lax.axis_index("seg")
    count = pts_size * seg_size
    bits = count.bit_length() - 1
    flat = pts * seg_size + seg
    segs = near_ref.shape[0]
    local = points_ref.shape[1]

    def seg_peer(d):
        return (group, pts, lax.rem(seg + d, seg_size))

    def bit_peer(k):
        bit = 1 << k
        other = flat + (1 - 2 * ((flat // bit) % 2)) * bit
        return (group, other // seg_size, other % seg_size)

    peers = [seg_peer(d) for d in range(1, seg_size)]
    peers += [bit_peer(k) for k in range(bits)]
    barrier = pltpu.get_barrier_semaphore()
    for peer in peers:
        pl.semaphore_signal(barrier, inc=1, device_id=peer, device_id_type=MESH)
    pl.semaphore_wait(barrier, len(peers))

    point_copies = []
    for d in range(1, seg_size):
        copy = pltpu.make_async_remote_copy(
            src_ref=points_ref, dst_ref=peer_points.at[d - 1],
            send_sem=point_send.at[d - 1], recv_sem=point_recv.at[d - 1],
            device_id=seg_peer(d), device_id_type=MESH)
        copy.start()
        point_copies.append(copy)

    def absorb(points, first, last):
        x = [points[k:k + 1, :] - centre_ref[k:k + 1, 0:1] for k in range(3)]
        rows = []
        for k in range(3):
            rows += right_rows(x[k])
        rows += right_rows(x[0] * x[0] + x[1] * x[1] + x[2] * x[2])
        rows += [jnp.ones((1, local), f32)] * 3
        rows += [jnp.zeros((1, local), f32)] * (DEPTH - len(rows))
        side[...] = jnp.concatenate(rows, axis=0).astype(bf16)

        def step(i, carry):
            for j in range(GROUP):
                rows = pl.ds(pl.multiple_of(i * (CHUNK * GROUP) + j * CHUNK, CHUNK), CHUNK)
                a2 = jnp.dot(near_ref[rows, :], side[...], preferred_element_type=f32)
                b2 = jnp.dot(far_ref[rows, :], side[...], preferred_element_type=f32)
                ra = lax.rsqrt(a2)
                rb = lax.rsqrt(b2)
                total = a2 * ra + b2 * rb
                factor = (ra + rb) * pl.reciprocal(total * total - 1.0, approx=True)
                hi = factor.astype(bf16)
                hi_buf[j * CHUNK:(j + 1) * CHUNK, :] = hi
                lo_buf[j * CHUNK:(j + 1) * CHUNK, :] = (factor - hi.astype(f32)).astype(bf16)
            cols = pl.ds(pl.multiple_of(i * (CHUNK * GROUP), CHUNK * GROUP), CHUNK * GROUP)
            both_acc[...] += jnp.dot(weight_ref[:, cols], hi_buf[...], preferred_element_type=f32)
            low_acc[...] += jnp.dot(weight_ref[0:6 * SNAPS, cols], lo_buf[...], preferred_element_type=f32)
            return carry

        lax.fori_loop(first, last, step, 0)
        return x

    def clear():
        both_acc[...] = jnp.zeros_like(both_acc)
        low_acc[...] = jnp.zeros_like(low_acc)

    def collect(x):
        g = both_acc[0:6 * SNAPS, :] + both_acc[6 * SNAPS:12 * SNAPS, :] + low_acc[...]
        g = [g[SNAPS * k:SNAPS * (k + 1), :] for k in range(6)]
        return [
            x[1] * g[2] - x[2] * g[1] + g[3],
            x[2] * g[0] - x[0] * g[2] + g[4],
            x[0] * g[1] - x[1] * g[0] + g[5],
        ]

    steps = segs // (CHUNK * GROUP)
    part_copies = []
    for d in range(1, seg_size):
        point_copies[d - 1].wait()
        clear()
        x = absorb(peer_points[d - 1], 0, steps)
        for c, block in enumerate(collect(x)):
            part_out[d - 1, SNAPS * c:SNAPS * (c + 1), :] = block
        copy = pltpu.make_async_remote_copy(
            src_ref=part_out.at[d - 1], dst_ref=part_in.at[d - 1],
            send_sem=part_send.at[d - 1], recv_sem=part_recv.at[d - 1],
            device_id=seg_peer(seg_size - d), device_id_type=MESH)
        copy.start()
        part_copies.append(copy)
    clear()
    x = absorb(points_ref[...], 0, steps)
    panel = jnp.concatenate(collect(x), axis=0)
    for d in range(1, seg_size):
        part_copies[d - 1].wait()
        panel = panel + part_in[d - 1]

    def all_sum(ref, slots, send, recv):
        for k in range(bits):
            copy = pltpu.make_async_remote_copy(
                src_ref=ref, dst_ref=slots.at[k], send_sem=send.at[k], recv_sem=recv.at[k],
                device_id=bit_peer(k), device_id_type=MESH)
            copy.start()
            copy.wait()
            ref[...] += slots[k]

    across = (((1,), (1,)), ((), ()))
    coeff_ref[...] = lax.dot_general(panel, modes_ref[...], across, precision=HIGH, preferred_element_type=f32)
    all_sum(coeff_ref, coeff_in, coeff_send, coeff_recv)
    proj = panel - jnp.dot(coeff_ref[...], modes_ref[...], precision=HIGH, preferred_element_type=f32)
    proj_ref[...] = proj
    gram_ref[...] = lax.dot_general(proj, proj, across, precision=HIGH, preferred_element_type=f32) * (
        1.0 / (count * local))
    all_sum(gram_ref, gram_in, gram_send, gram_recv)


def solve_kernel(gram_ref, proj_ref, factor_ref, basis_ref):
    order = gram_ref.shape[0]
    tiles = order // 8
    gram = [gram_ref[8 * t:8 * t + 8, :] for t in range(tiles)]
    right = [proj_ref[8 * t:8 * t + 8, :] for t in range(tiles)]
    row = lax.broadcasted_iota(jnp.int32, (8, 1), 0)
    for k in range(order):
        at, r = k // 8, k % 8
        line = gram[at][r:r + 1, :]
        inv = lax.rsqrt(line[:, k:k + 1])
        line = line * inv
        side = right[at][r:r + 1, :] * inv
        for t in range(at, tiles):
            col = gram[t][:, k:k + 1] * inv
            if t == at:
                col = jnp.where(row > r, col, 0.0)
            gram[t] = gram[t] - col * line
            right[t] = right[t] - col * side
        gram[at] = jnp.where(row == r, line, gram[at])
        right[at] = jnp.where(row == r, side, right[at])
    col = lax.broadcasted_iota(jnp.int32, (8, order), 1)
    for t in range(tiles):
        factor_ref[8 * t:8 * t + 8, :] = jnp.where(col >= row + 8 * t, gram[t], 0.0)
        basis_ref[8 * t:8 * t + 8, :] = right[t]


def body(pts_size, seg_size, field_points, wake_nodes, trail_node, strength, core_square, snapshot, stored_modes):
    segs = wake_nodes.shape[1]
    local = field_points.shape[1]
    modes = stored_modes.shape[0]
    rank = 3 * SNAPS
    bits = (pts_size * seg_size).bit_length() - 1
    shape = jax.ShapeDtypeStruct
    vmem = pl.BlockSpec(memory_space=pltpu.VMEM)
    near, far, weight, centre = pl.pallas_call(
        prep_kernel,
        out_shape=(
            shape((segs, DEPTH), bf16), shape((segs, DEPTH), bf16),
            shape((12 * SNAPS, segs), bf16), shape((3, 128), f32)),
        in_specs=[vmem] * 5,
        out_specs=(vmem,) * 4,
        scratch_shapes=[pltpu.VMEM((3, segs), f32)],
        compiler_params=pltpu.CompilerParams(vmem_limit_bytes=40 * 1024 * 1024),
        name="prep",
    )(wake_nodes, trail_node.reshape(segs // 128, 128), strength[None], core_square[None], snapshot[None])
    peers = seg_size - 1
    dma = pltpu.SemaphoreType.DMA
    coeffs, gram, proj = pl.pallas_call(
        functools.partial(main_kernel, pts_size, seg_size),
        out_shape=(shape((rank, modes), f32), shape((rank, rank), f32), shape((rank, local), f32)),
        in_specs=[vmem] * 6,
        out_specs=(vmem,) * 3,
        scratch_shapes=[
            pltpu.VMEM((peers, 3, local), f32),
            pltpu.VMEM((peers, rank, local), f32),
            pltpu.VMEM((peers, rank, local), f32),
            pltpu.VMEM((12 * SNAPS, local), f32),
            pltpu.VMEM((6 * SNAPS, local), f32),
            pltpu.VMEM((DEPTH, local), bf16),
            pltpu.VMEM((CHUNK * GROUP, local), bf16),
            pltpu.VMEM((CHUNK * GROUP, local), bf16),
            pltpu.VMEM((bits, rank, modes), f32),
            pltpu.VMEM((bits, rank, rank), f32),
            dma((peers,)), dma((peers,)), dma((peers,)), dma((peers,)),
            dma((bits,)), dma((bits,)), dma((bits,)), dma((bits,)),
        ],
        compiler_params=pltpu.CompilerParams(
            collective_id=0, has_side_effects=True, vmem_limit_bytes=40 * 1024 * 1024),
        name="main",
    )(field_points, near, far, weight, centre, stored_modes)
    factor, basis = pl.pallas_call(
        solve_kernel,
        out_shape=(shape((rank, rank), f32), shape((rank, local), f32)),
        in_specs=[vmem] * 2,
        out_specs=(vmem,) * 2,
        name="solve",
    )(gram, proj)
    return coeffs.T, factor, basis


def solution(mesh):
    return jax.shard_map(
        functools.partial(body, mesh.shape["pts"], mesh.shape["seg"]),
        mesh=mesh,
        in_specs=(
            P(None, ("groups", "pts", "seg")),
            P(None, ("groups", "seg")),
            P(("groups", "seg")),
            P(("groups", "seg")),
            P(("groups", "seg")),
            P(("groups", "seg")),
            P(None, ("groups", "pts", "seg")),
        ),
        out_specs=(P("groups", None), P("groups", None), P(None, ("groups", "pts", "seg"))),
        check_vma=False,
    )
```

```python
import functools
import math

import jax
import jax.numpy as jnp
from jax import lax
from jax.experimental import pallas as pl
from jax.experimental.pallas import tpu as pltpu
from jax.sharding import PartitionSpec as P

SNAPS = 16
HIGH = lax.Precision.HIGHEST
MESH = pl.DeviceIdType.MESH
DEPTH = 32
CHUNK = 256
GROUP = 8
f32 = jnp.float32
bf16 = jnp.bfloat16


def split3(v):
    hi = v.astype(bf16).astype(f32)
    rest = v - hi
    mid = rest.astype(bf16).astype(f32)
    return hi, mid, (rest - mid).astype(bf16).astype(f32)


def left_rows(v):
    hi, mid, lo = split3(v)
    return [hi, hi, mid, hi, lo, mid]


def right_rows(v):
    hi, mid, lo = split3(v)
    return [hi, mid, hi, lo, hi, mid]


def prep_kernel(nodes_in, trail_in, strength_in, core_in, snap_in,
                near_ref, far_ref, weight_ref, centre_ref,
                nodes_ref, trail_ref, strength_ref, core_ref, snap_ref, head_ref, sems):
    pairs = ((nodes_in, nodes_ref), (trail_in, trail_ref), (strength_in, strength_ref),
             (core_in, core_ref), (snap_in, snap_ref))
    copies = [pltpu.make_async_copy(a, b, sems.at[i]) for i, (a, b) in enumerate(pairs)]
    for copy in copies:
        copy.start()
    copies[0].wait()
    copies[1].wait()
    segs = nodes_ref.shape[1]
    rows = segs // 128
    nodes = nodes_ref[...]
    centre = jnp.sum(nodes, axis=1, keepdims=True) * (1.0 / segs)
    centre_ref[...] = jnp.broadcast_to(centre, centre_ref.shape)

    tiles = rows // 8
    high = [trail_ref[8 * r:8 * r + 8, :] // 128 for r in range(tiles)]
    low = [trail_ref[8 * r:8 * r + 8, :] % 128 for r in range(tiles)]

    def look(h, found):
        cols = pl.ds(pl.multiple_of(h * 128, 128), 128)
        out = list(found)
        table = [jnp.broadcast_to(nodes_ref[k:k + 1, cols], (8, 128)) for k in range(3)]
        for r in range(tiles):
            here = high[r] == h
            for k in range(3):
                got = jnp.take_along_axis(table[k], low[r], axis=1, mode="promise_in_bounds")
                out[3 * r + k] = jnp.where(here, got, out[3 * r + k])
        return tuple(out)

    found = lax.fori_loop(0, rows, look, tuple(jnp.zeros((8, 128), f32) for _ in range(3 * tiles)))
    for r in range(tiles):
        for k in range(3):
            for i in range(8):
                at = (8 * r + i) * 128
                head_ref[k:k + 1, at:at + 128] = found[3 * r + k][i:i + 1, :]

    for copy in copies[2:]:
        copy.wait()
    width = 1024
    zero = jnp.zeros((1, width), f32)
    levels = lax.broadcasted_iota(jnp.int32, (SNAPS, width), 0)

    def fill(b, carry):
        cols = pl.ds(pl.multiple_of(b * width, 128), width)
        t = [nodes_ref[k:k + 1, cols] - centre[k:k + 1, :] for k in range(3)]
        h = [head_ref[k:k + 1, cols] - centre[k:k + 1, :] for k in range(3)]
        core = core_ref[:, cols]
        d = [t[k] - h[k] for k in range(3)]
        q = 2.0 * core + (d[0] * d[0] + d[1] * d[1] + d[2] * d[2])
        g = 1.0 / q
        for ref, e in ((near_ref, t), (far_ref, h)):
            square = e[0] * e[0] + e[1] * e[1] + e[2] * e[2] + core
            parts = []
            for k in range(3):
                parts += left_rows(-2.0 * g * e[k])
            parts += left_rows(g) + list(split3(g * square))
            parts += [zero] * (DEPTH - len(parts))
            packed = jnp.concatenate(parts, axis=0)
            ref[pl.ds(pl.multiple_of(b * width, 128), width), :] = packed.T.astype(bf16)
        scale = strength_ref[:, cols] * (2.0 / (4.0 * math.pi)) * g * jnp.sqrt(g)
        v = d + [t[1] * h[2] - t[2] * h[1], t[2] * h[0] - t[0] * h[2], t[0] * h[1] - t[1] * h[0]]
        mine = snap_ref[:, cols] == levels
        for k in range(6):
            value = v[k] * scale
            hi = value.astype(bf16).astype(f32)
            lo = value - hi
            at = SNAPS * k
            weight_ref[at:at + SNAPS, cols] = jnp.where(mine, hi, 0.0).astype(bf16)
            weight_ref[6 * SNAPS + at:6 * SNAPS + at + SNAPS, cols] = jnp.where(mine, lo, 0.0).astype(bf16)
        return carry

    lax.fori_loop(0, segs // width, fill, 0)


def main_kernel(pts_size, seg_size, points_ref, near_ref, far_ref, weight_ref, centre_ref, modes_in,
                coeff_ref, gram_ref, proj_ref,
                points, modes_ref, peer_points, part_out, part_in, own_both, own_low, both_acc, low_acc,
                side, hi_buf, lo_buf, coeff_part, coeff_seg, coeff_pts, coeff_mine, coeff_all, gram_part, gram_seg, gram_pts,
                local_sem, point_send, point_recv, part_send, part_recv,
                send_a, recv_a, send_b, recv_b, send_c, recv_c, send_d, recv_d, send_e, recv_e):
    group = lax.axis_index("groups")
    pts = lax.axis_index("pts")
    seg = lax.axis_index("seg")
    segs = near_ref.shape[0]
    local = points_ref.shape[1]
    rank = 3 * SNAPS
    width = modes_in.shape[0] // seg_size

    def seg_peer(d):
        return (group, pts, lax.rem(seg + d, seg_size))

    def pts_peer(d):
        return (group, lax.rem(pts + d, pts_size), seg)

    barrier = pltpu.get_barrier_semaphore()
    peers = [seg_peer(d) for d in range(1, seg_size)] + [pts_peer(d) for d in range(1, pts_size)]
    for peer in peers:
        pl.semaphore_signal(barrier, inc=1, device_id=peer, device_id_type=MESH)

    get_points = pltpu.make_async_copy(points_ref, points, local_sem.at[0])
    get_points.start()
    get_modes = pltpu.make_async_copy(modes_in, modes_ref, local_sem.at[1])
    get_modes.start()

    def send(src, dst, send_sem, recv_sem, peer):
        copy = pltpu.make_async_remote_copy(
            src_ref=src, dst_ref=dst, send_sem=send_sem, recv_sem=recv_sem,
            device_id=peer, device_id_type=MESH)
        copy.start()
        return copy

    def place(raw):
        x = [raw[k:k + 1, :] - centre_ref[k:k + 1, 0:1] for k in range(3)]
        rows = []
        for k in range(3):
            rows += right_rows(x[k])
        rows += right_rows(x[0] * x[0] + x[1] * x[1] + x[2] * x[2])
        rows += [jnp.ones((1, local), f32)] * 3
        rows += [jnp.zeros((1, local), f32)] * (DEPTH - len(rows))
        side[...] = jnp.concatenate(rows, axis=0).astype(bf16)
        return x

    def absorb(both, low, first, last):
        def step(i, carry):
            for j in range(GROUP):
                rows = pl.ds(pl.multiple_of(i * (CHUNK * GROUP) + j * CHUNK, CHUNK), CHUNK)
                a2 = jnp.dot(near_ref[rows, :], side[...], preferred_element_type=f32)
                b2 = jnp.dot(far_ref[rows, :], side[...], preferred_element_type=f32)
                ra = lax.rsqrt(a2)
                rb = lax.rsqrt(b2)
                total = a2 * ra + b2 * rb
                factor = (ra + rb) * pl.reciprocal(total * total - 1.0, approx=True)
                hi = factor.astype(bf16)
                hi_buf[j * CHUNK:(j + 1) * CHUNK, :] = hi
                lo_buf[j * CHUNK:(j + 1) * CHUNK, :] = (factor - hi.astype(f32)).astype(bf16)
            cols = pl.ds(pl.multiple_of(i * (CHUNK * GROUP), CHUNK * GROUP), CHUNK * GROUP)
            both[...] += jnp.dot(weight_ref[:, cols], hi_buf[...], preferred_element_type=f32)
            low[...] += jnp.dot(weight_ref[0:6 * SNAPS, cols], lo_buf[...], preferred_element_type=f32)
            return carry

        lax.fori_loop(first, last, step, 0)

    def collect(x, both, low):
        g = both[0:6 * SNAPS, :] + both[6 * SNAPS:12 * SNAPS, :] + low[...]
        g = [g[SNAPS * k:SNAPS * (k + 1), :] for k in range(6)]
        return [
            x[1] * g[2] - x[2] * g[1] + g[3],
            x[2] * g[0] - x[0] * g[2] + g[4],
            x[0] * g[1] - x[1] * g[0] + g[5],
        ]

    steps = segs // (CHUNK * GROUP)
    cut = (steps // 4, steps - steps // 4)
    own_both[...] = jnp.zeros_like(own_both)
    own_low[...] = jnp.zeros_like(own_low)
    get_points.wait()
    place(points[...])
    absorb(own_both, own_low, 0, cut[0])
    pl.semaphore_wait(barrier, len(peers))
    point_copies = [
        send(points, peer_points.at[d - 1], point_send.at[d - 1], point_recv.at[d - 1], seg_peer(d))
        for d in range(1, seg_size)]
    absorb(own_both, own_low, cut[0], cut[1])

    part_copies = []
    for d in range(1, seg_size):
        point_copies[d - 1].wait()
        both_acc[...] = jnp.zeros_like(both_acc)
        low_acc[...] = jnp.zeros_like(low_acc)
        x = place(peer_points[d - 1])
        absorb(both_acc, low_acc, 0, steps)
        for c, block in enumerate(collect(x, both_acc, low_acc)):
            part_out[d - 1, SNAPS * c:SNAPS * (c + 1), :] = block
        part_copies.append(send(
            part_out.at[d - 1], part_in.at[d - 1], part_send.at[d - 1], part_recv.at[d - 1],
            seg_peer(seg_size - d)))
    x = place(points[...])
    absorb(own_both, own_low, cut[1], steps)
    panel = jnp.concatenate(collect(x, own_both, own_low), axis=0)
    for d in range(1, seg_size):
        part_copies[d - 1].wait()
        panel = panel + part_in[d - 1]
    get_modes.wait()

    def spread(src_of, dst, mine, size, peer_of, send_sem, recv_sem):
        copies = [
            send(src_of(d), dst.at[mine], send_sem.at[d - 1], recv_sem.at[d - 1], peer_of(d))
            for d in range(1, size)]
        for copy in copies:
            copy.wait()

    def added(slots, size):
        total = slots[0]
        for i in range(1, size):
            total = total + slots[i]
        return total

    across = (((1,), (1,)), ((), ()))
    for q in range(seg_size):
        coeff_part[q] = lax.dot_general(
            panel, modes_ref[q * width:(q + 1) * width, :], across, precision=HIGH, preferred_element_type=f32)
    coeff_seg[seg] = coeff_part[seg]
    spread(lambda d: coeff_part.at[lax.rem(seg + d, seg_size)], coeff_seg, seg, seg_size, seg_peer, send_a, recv_a)
    coeff_mine[0] = added(coeff_seg, seg_size)
    coeff_pts[pts] = coeff_mine[0]
    spread(lambda d: coeff_mine.at[0], coeff_pts, pts, pts_size, pts_peer, send_b, recv_b)
    coeff_mine[1] = added(coeff_pts, pts_size)
    coeff_all[seg] = coeff_mine[1]
    spread(lambda d: coeff_mine.at[1], coeff_all, seg, seg_size, seg_peer, send_c, recv_c)
    proj = panel
    for q in range(seg_size):
        block = coeff_all[q]
        coeff_ref[:, q * width:(q + 1) * width] = block
        proj = proj - jnp.dot(
            block, modes_ref[q * width:(q + 1) * width, :], precision=HIGH, preferred_element_type=f32)
    proj_ref[...] = proj
    gram_part[0] = lax.dot_general(proj, proj, across, precision=HIGH, preferred_element_type=f32) * (
        1.0 / (pts_size * seg_size * local))
    gram_seg[seg] = gram_part[0]
    spread(lambda d: gram_part.at[0], gram_seg, seg, seg_size, seg_peer, send_d, recv_d)
    gram_part[1] = added(gram_seg, seg_size)
    gram_pts[pts] = gram_part[1]
    spread(lambda d: gram_part.at[1], gram_pts, pts, pts_size, pts_peer, send_e, recv_e)
    gram_ref[...] = added(gram_pts, pts_size)


def solve_kernel(gram_ref, proj_ref, factor_ref, basis_ref):
    order = gram_ref.shape[0]
    tiles = order // 8
    gram = [gram_ref[8 * t:8 * t + 8, :] for t in range(tiles)]
    right = [proj_ref[8 * t:8 * t + 8, :] for t in range(tiles)]
    row = lax.broadcasted_iota(jnp.int32, (8, 1), 0)
    for k in range(order):
        at, r = k // 8, k % 8
        line = gram[at][r:r + 1, :]
        inv = lax.rsqrt(line[:, k:k + 1])
        line = line * inv
        side = right[at][r:r + 1, :] * inv
        for t in range(at, tiles):
            col = gram[t][:, k:k + 1] * inv
            if t == at:
                col = jnp.where(row > r, col, 0.0)
            gram[t] = gram[t] - col * line
            right[t] = right[t] - col * side
        gram[at] = jnp.where(row == r, line, gram[at])
        right[at] = jnp.where(row == r, side, right[at])
    col = lax.broadcasted_iota(jnp.int32, (8, order), 1)
    for t in range(tiles):
        factor_ref[8 * t:8 * t + 8, :] = jnp.where(col >= row + 8 * t, gram[t], 0.0)
        basis_ref[8 * t:8 * t + 8, :] = right[t]


def body(pts_size, seg_size, field_points, wake_nodes, trail_node, strength, core_square, snapshot, stored_modes):
    segs = wake_nodes.shape[1]
    local = field_points.shape[1]
    modes = stored_modes.shape[0]
    rank = 3 * SNAPS
    shape = jax.ShapeDtypeStruct
    vmem = pl.BlockSpec(memory_space=pltpu.VMEM)
    hbm = pl.BlockSpec(memory_space=pl.ANY)
    dma = pltpu.SemaphoreType.DMA
    near, far, weight, centre = pl.pallas_call(
        prep_kernel,
        out_shape=(
            shape((segs, DEPTH), bf16), shape((segs, DEPTH), bf16),
            shape((12 * SNAPS, segs), bf16), shape((3, 128), f32)),
        in_specs=[hbm] * 5,
        out_specs=(vmem,) * 4,
        scratch_shapes=[
            pltpu.VMEM((3, segs), f32), pltpu.VMEM((segs // 128, 128), jnp.int32),
            pltpu.VMEM((1, segs), f32), pltpu.VMEM((1, segs), f32), pltpu.VMEM((1, segs), jnp.int32),
            pltpu.VMEM((3, segs), f32), dma((5,))],
        compiler_params=pltpu.CompilerParams(vmem_limit_bytes=50 * 1024 * 1024),
        name="prep",
    )(wake_nodes, trail_node.reshape(segs // 128, 128), strength[None], core_square[None], snapshot[None])
    peers = seg_size - 1
    far_peers = pts_size - 1
    width = modes // seg_size
    coeffs, gram, proj = pl.pallas_call(
        functools.partial(main_kernel, pts_size, seg_size),
        out_shape=(shape((rank, modes), f32), shape((rank, rank), f32), shape((rank, local), f32)),
        in_specs=[hbm] + [vmem] * 4 + [hbm],
        out_specs=(vmem,) * 3,
        scratch_shapes=[
            pltpu.VMEM((3, local), f32),
            pltpu.VMEM((modes, local), f32),
            pltpu.VMEM((peers, 3, local), f32),
            pltpu.VMEM((peers, rank, local), f32),
            pltpu.VMEM((peers, rank, local), f32),
            pltpu.VMEM((12 * SNAPS, local), f32),
            pltpu.VMEM((6 * SNAPS, local), f32),
            pltpu.VMEM((12 * SNAPS, local), f32),
            pltpu.VMEM((6 * SNAPS, local), f32),
            pltpu.VMEM((DEPTH, local), bf16),
            pltpu.VMEM((CHUNK * GROUP, local), bf16),
            pltpu.VMEM((CHUNK * GROUP, local), bf16),
            pltpu.VMEM((seg_size, rank, width), f32),
            pltpu.VMEM((seg_size, rank, width), f32),
            pltpu.VMEM((pts_size, rank, width), f32),
            pltpu.VMEM((2, rank, width), f32),
            pltpu.VMEM((seg_size, rank, width), f32),
            pltpu.VMEM((2, rank, rank), f32),
            pltpu.VMEM((seg_size, rank, rank), f32),
            pltpu.VMEM((pts_size, rank, rank), f32),
            dma((2,)),
            dma((peers,)), dma((peers,)), dma((peers,)), dma((peers,)),
            dma((peers,)), dma((peers,)), dma((far_peers,)), dma((far_peers,)), dma((peers,)), dma((peers,)),
            dma((peers,)), dma((peers,)), dma((far_peers,)), dma((far_peers,)),
        ],
        compiler_params=pltpu.CompilerParams(
            collective_id=0, has_side_effects=True, vmem_limit_bytes=50 * 1024 * 1024),
        name="main",
    )(field_points, near, far, weight, centre, stored_modes)
    factor, basis = pl.pallas_call(
        solve_kernel,
        out_shape=(shape((rank, rank), f32), shape((rank, local), f32)),
        in_specs=[vmem] * 2,
        out_specs=(vmem,) * 2,
        name="solve",
    )(gram, proj)
    return coeffs.T, factor, basis


def solution(mesh):
    return jax.shard_map(
        functools.partial(body, mesh.shape["pts"], mesh.shape["seg"]),
        mesh=mesh,
        in_specs=(
            P(None, ("groups", "pts", "seg")),
            P(None, ("groups", "seg")),
            P(("groups", "seg")),
            P(("groups", "seg")),
            P(("groups", "seg")),
            P(("groups", "seg")),
            P(None, ("groups", "pts", "seg")),
        ),
        out_specs=(P("groups", None), P("groups", None), P(None, ("groups", "pts", "seg"))),
        check_vma=False,
    )
```

```python
import functools
import math

import jax
import jax.numpy as jnp
from jax import lax
from jax.experimental import pallas as pl
from jax.experimental.pallas import tpu as pltpu
from jax.sharding import PartitionSpec as P

SNAPS = 16
HIGH = lax.Precision.HIGHEST
MESH = pl.DeviceIdType.MESH
DEPTH = 32
CHUNK = 256
GROUP = 8
f32 = jnp.float32
bf16 = jnp.bfloat16


def split3(v):
    hi = v.astype(bf16).astype(f32)
    rest = v - hi
    mid = rest.astype(bf16).astype(f32)
    return hi, mid, (rest - mid).astype(bf16).astype(f32)


def left_rows(v):
    hi, mid, lo = split3(v)
    return [hi, hi, mid, hi, lo, mid]


def right_rows(v):
    hi, mid, lo = split3(v)
    return [hi, mid, hi, lo, hi, mid]


def prepare(nodes_in, trail_in, strength_in, core_in, snap_in,
                near_ref, far_ref, weight_ref, centre_ref,
                nodes_ref, trail_ref, strength_ref, core_ref, snap_ref, head_ref, sems):
    pairs = ((nodes_in, nodes_ref), (trail_in, trail_ref), (strength_in, strength_ref),
             (core_in, core_ref), (snap_in, snap_ref))
    copies = [pltpu.make_async_copy(a, b, sems.at[i]) for i, (a, b) in enumerate(pairs)]
    for copy in copies:
        copy.start()
    copies[0].wait()
    copies[1].wait()
    segs = nodes_ref.shape[1]
    rows = segs // 128
    nodes = nodes_ref[...]
    centre = jnp.sum(nodes, axis=1, keepdims=True) * (1.0 / segs)
    centre_ref[...] = jnp.broadcast_to(centre, centre_ref.shape)

    tiles = rows // 8
    high = [trail_ref[8 * r:8 * r + 8, :] // 128 for r in range(tiles)]
    low = [trail_ref[8 * r:8 * r + 8, :] % 128 for r in range(tiles)]

    def look(h, found):
        cols = pl.ds(pl.multiple_of(h * 128, 128), 128)
        out = list(found)
        table = [jnp.broadcast_to(nodes_ref[k:k + 1, cols], (8, 128)) for k in range(3)]
        for r in range(tiles):
            here = high[r] == h
            for k in range(3):
                got = jnp.take_along_axis(table[k], low[r], axis=1, mode="promise_in_bounds")
                out[3 * r + k] = jnp.where(here, got, out[3 * r + k])
        return tuple(out)

    found = lax.fori_loop(0, rows, look, tuple(jnp.zeros((8, 128), f32) for _ in range(3 * tiles)))
    for r in range(tiles):
        for k in range(3):
            for i in range(8):
                at = (8 * r + i) * 128
                head_ref[k:k + 1, at:at + 128] = found[3 * r + k][i:i + 1, :]

    for copy in copies[2:]:
        copy.wait()
    width = 1024
    zero = jnp.zeros((1, width), f32)
    levels = lax.broadcasted_iota(jnp.int32, (SNAPS, width), 0)

    def fill(b, carry):
        cols = pl.ds(pl.multiple_of(b * width, 128), width)
        t = [nodes_ref[k:k + 1, cols] - centre[k:k + 1, :] for k in range(3)]
        h = [head_ref[k:k + 1, cols] - centre[k:k + 1, :] for k in range(3)]
        core = core_ref[:, cols]
        d = [t[k] - h[k] for k in range(3)]
        q = 2.0 * core + (d[0] * d[0] + d[1] * d[1] + d[2] * d[2])
        g = 1.0 / q
        for ref, e in ((near_ref, t), (far_ref, h)):
            square = e[0] * e[0] + e[1] * e[1] + e[2] * e[2] + core
            parts = []
            for k in range(3):
                parts += left_rows(-2.0 * g * e[k])
            parts += left_rows(g) + list(split3(g * square))
            parts += [zero] * (DEPTH - len(parts))
            packed = jnp.concatenate(parts, axis=0)
            ref[pl.ds(pl.multiple_of(b * width, 128), width), :] = packed.T.astype(bf16)
        scale = strength_ref[:, cols] * (2.0 / (4.0 * math.pi)) * g * jnp.sqrt(g)
        v = d + [t[1] * h[2] - t[2] * h[1], t[2] * h[0] - t[0] * h[2], t[0] * h[1] - t[1] * h[0]]
        mine = snap_ref[:, cols] == levels
        for k in range(6):
            value = v[k] * scale
            hi = value.astype(bf16).astype(f32)
            lo = value - hi
            at = SNAPS * k
            weight_ref[at:at + SNAPS, cols] = jnp.where(mine, hi, 0.0).astype(bf16)
            weight_ref[6 * SNAPS + at:6 * SNAPS + at + SNAPS, cols] = jnp.where(mine, lo, 0.0).astype(bf16)
        return carry

    lax.fori_loop(0, segs // width, fill, 0)


def main_kernel(pts_size, seg_size, points_ref, nodes_in, trail_in, strength_in, core_in, snap_in, modes_in,
                coeff_ref, gram_ref, proj_ref,
                near_ref, far_ref, weight_ref, centre_ref,
                nodes_ref, trail_ref, strength_ref, core_ref, snap_ref, head_ref, prep_sems,
                points, modes_ref, peer_points, part_out, part_in, own_both, own_low, both_acc, low_acc,
                side, hi_buf, lo_buf, coeff_part, coeff_seg, coeff_pts, coeff_mine, coeff_all, gram_part, gram_seg, gram_pts,
                local_sem, point_send, point_recv, part_send, part_recv,
                send_a, recv_a, send_b, recv_b, send_c, recv_c, send_d, recv_d, send_e, recv_e):
    group = lax.axis_index("groups")
    pts = lax.axis_index("pts")
    seg = lax.axis_index("seg")
    segs = near_ref.shape[0]
    local = points_ref.shape[1]
    rank = 3 * SNAPS
    width = modes_in.shape[0] // seg_size

    def seg_peer(d):
        return (group, pts, lax.rem(seg + d, seg_size))

    def pts_peer(d):
        return (group, lax.rem(pts + d, pts_size), seg)

    barrier = pltpu.get_barrier_semaphore()
    peers = [seg_peer(d) for d in range(1, seg_size)] + [pts_peer(d) for d in range(1, pts_size)]
    for peer in peers:
        pl.semaphore_signal(barrier, inc=1, device_id=peer, device_id_type=MESH)

    get_points = pltpu.make_async_copy(points_ref, points, local_sem.at[0])
    get_points.start()
    get_modes = pltpu.make_async_copy(modes_in, modes_ref, local_sem.at[1])
    get_modes.start()
    prepare(nodes_in, trail_in, strength_in, core_in, snap_in, near_ref, far_ref, weight_ref, centre_ref,
            nodes_ref, trail_ref, strength_ref, core_ref, snap_ref, head_ref, prep_sems)

    def send(src, dst, send_sem, recv_sem, peer):
        copy = pltpu.make_async_remote_copy(
            src_ref=src, dst_ref=dst, send_sem=send_sem, recv_sem=recv_sem,
            device_id=peer, device_id_type=MESH)
        copy.start()
        return copy

    def place(raw):
        x = [raw[k:k + 1, :] - centre_ref[k:k + 1, 0:1] for k in range(3)]
        rows = []
        for k in range(3):
            rows += right_rows(x[k])
        rows += right_rows(x[0] * x[0] + x[1] * x[1] + x[2] * x[2])
        rows += [jnp.ones((1, local), f32)] * 3
        rows += [jnp.zeros((1, local), f32)] * (DEPTH - len(rows))
        side[...] = jnp.concatenate(rows, axis=0).astype(bf16)
        return x

    def absorb(both, low, first, last):
        def step(i, carry):
            for j in range(GROUP):
                rows = pl.ds(pl.multiple_of(i * (CHUNK * GROUP) + j * CHUNK, CHUNK), CHUNK)
                a2 = jnp.dot(near_ref[rows, :], side[...], preferred_element_type=f32)
                b2 = jnp.dot(far_ref[rows, :], side[...], preferred_element_type=f32)
                ra = lax.rsqrt(a2)
                rb = lax.rsqrt(b2)
                total = a2 * ra + b2 * rb
                factor = (ra + rb) * pl.reciprocal(total * total - 1.0, approx=True)
                hi = factor.astype(bf16)
                hi_buf[j * CHUNK:(j + 1) * CHUNK, :] = hi
                lo_buf[j * CHUNK:(j + 1) * CHUNK, :] = (factor - hi.astype(f32)).astype(bf16)
            cols = pl.ds(pl.multiple_of(i * (CHUNK * GROUP), CHUNK * GROUP), CHUNK * GROUP)
            both[...] += jnp.dot(weight_ref[:, cols], hi_buf[...], preferred_element_type=f32)
            low[...] += jnp.dot(weight_ref[0:6 * SNAPS, cols], lo_buf[...], preferred_element_type=f32)
            return carry

        lax.fori_loop(first, last, step, 0)

    def collect(x, both, low):
        g = both[0:6 * SNAPS, :] + both[6 * SNAPS:12 * SNAPS, :] + low[...]
        g = [g[SNAPS * k:SNAPS * (k + 1), :] for k in range(6)]
        return [
            x[1] * g[2] - x[2] * g[1] + g[3],
            x[2] * g[0] - x[0] * g[2] + g[4],
            x[0] * g[1] - x[1] * g[0] + g[5],
        ]

    steps = segs // (CHUNK * GROUP)
    cut = (steps // 4, steps - steps // 4)
    own_both[...] = jnp.zeros_like(own_both)
    own_low[...] = jnp.zeros_like(own_low)
    get_points.wait()
    place(points[...])
    absorb(own_both, own_low, 0, cut[0])
    pl.semaphore_wait(barrier, len(peers))
    point_copies = [
        send(points, peer_points.at[d - 1], point_send.at[d - 1], point_recv.at[d - 1], seg_peer(d))
        for d in range(1, seg_size)]
    absorb(own_both, own_low, cut[0], cut[1])

    part_copies = []
    for d in range(1, seg_size):
        point_copies[d - 1].wait()
        both_acc[...] = jnp.zeros_like(both_acc)
        low_acc[...] = jnp.zeros_like(low_acc)
        x = place(peer_points[d - 1])
        absorb(both_acc, low_acc, 0, steps)
        for c, block in enumerate(collect(x, both_acc, low_acc)):
            part_out[d - 1, SNAPS * c:SNAPS * (c + 1), :] = block
        part_copies.append(send(
            part_out.at[d - 1], part_in.at[d - 1], part_send.at[d - 1], part_recv.at[d - 1],
            seg_peer(seg_size - d)))
    x = place(points[...])
    absorb(own_both, own_low, cut[1], steps)
    panel = jnp.concatenate(collect(x, own_both, own_low), axis=0)
    for d in range(1, seg_size):
        part_copies[d - 1].wait()
        panel = panel + part_in[d - 1]
    get_modes.wait()

    def spread(src_of, dst, mine, size, peer_of, send_sem, recv_sem):
        copies = [
            send(src_of(d), dst.at[mine], send_sem.at[d - 1], recv_sem.at[d - 1], peer_of(d))
            for d in range(1, size)]
        for copy in copies:
            copy.wait()

    def added(slots, size):
        total = slots[0]
        for i in range(1, size):
            total = total + slots[i]
        return total

    across = (((1,), (1,)), ((), ()))
    for q in range(seg_size):
        coeff_part[q] = lax.dot_general(
            panel, modes_ref[q * width:(q + 1) * width, :], across, precision=HIGH, preferred_element_type=f32)
    coeff_seg[seg] = coeff_part[seg]
    spread(lambda d: coeff_part.at[lax.rem(seg + d, seg_size)], coeff_seg, seg, seg_size, seg_peer, send_a, recv_a)
    coeff_mine[0] = added(coeff_seg, seg_size)
    coeff_pts[pts] = coeff_mine[0]
    spread(lambda d: coeff_mine.at[0], coeff_pts, pts, pts_size, pts_peer, send_b, recv_b)
    coeff_mine[1] = added(coeff_pts, pts_size)
    coeff_all[seg] = coeff_mine[1]
    spread(lambda d: coeff_mine.at[1], coeff_all, seg, seg_size, seg_peer, send_c, recv_c)
    proj = panel
    for q in range(seg_size):
        block = coeff_all[q]
        coeff_ref[:, q * width:(q + 1) * width] = block
        proj = proj - jnp.dot(
            block, modes_ref[q * width:(q + 1) * width, :], precision=HIGH, preferred_element_type=f32)
    proj_ref[...] = proj
    gram_part[0] = lax.dot_general(proj, proj, across, precision=HIGH, preferred_element_type=f32) * (
        1.0 / (pts_size * seg_size * local))
    gram_seg[seg] = gram_part[0]
    spread(lambda d: gram_part.at[0], gram_seg, seg, seg_size, seg_peer, send_d, recv_d)
    gram_part[1] = added(gram_seg, seg_size)
    gram_pts[pts] = gram_part[1]
    spread(lambda d: gram_part.at[1], gram_pts, pts, pts_size, pts_peer, send_e, recv_e)
    gram_ref[...] = added(gram_pts, pts_size)


def solve_kernel(gram_ref, proj_ref, factor_ref, basis_ref):
    order = gram_ref.shape[0]
    tiles = order // 8
    gram = [gram_ref[8 * t:8 * t + 8, :] for t in range(tiles)]
    right = [proj_ref[8 * t:8 * t + 8, :] for t in range(tiles)]
    row = lax.broadcasted_iota(jnp.int32, (8, 1), 0)
    width = proj_ref.shape[1]
    lanes = min(width, 128)
    for k in range(order):
        at, r = k // 8, k % 8
        cols = [None] * at + [jnp.broadcast_to(gram[t][:, k:k + 1], (8, lanes)) for t in range(at, tiles)]
        pivot = cols[at][r:r + 1, :]
        inv = 1.0 / pivot
        root = lax.rsqrt(pivot)
        line = gram[at][r:r + 1, :]
        side = right[at][r:r + 1, :]
        step = line * inv[:, :order]
        push = side * jnp.concatenate([inv] * (width // lanes), axis=1)
        cols[at] = jnp.where(row > r, cols[at], 0.0)
        for t in range(at, tiles):
            gram[t] = gram[t] - cols[t][:, :order] * step
            right[t] = right[t] - jnp.concatenate([cols[t]] * (width // lanes), axis=1) * push
        gram[at] = jnp.where(row == r, line * root[:, :order], gram[at])
        right[at] = jnp.where(row == r, side * jnp.concatenate([root] * (width // lanes), axis=1), right[at])
    col = lax.broadcasted_iota(jnp.int32, (8, order), 1)
    for t in range(tiles):
        factor_ref[8 * t:8 * t + 8, :] = jnp.where(col >= row + 8 * t, gram[t], 0.0)
        basis_ref[8 * t:8 * t + 8, :] = right[t]


def body(pts_size, seg_size, field_points, wake_nodes, trail_node, strength, core_square, snapshot, stored_modes):
    segs = wake_nodes.shape[1]
    local = field_points.shape[1]
    modes = stored_modes.shape[0]
    rank = 3 * SNAPS
    shape = jax.ShapeDtypeStruct
    vmem = pl.BlockSpec(memory_space=pltpu.VMEM)
    hbm = pl.BlockSpec(memory_space=pl.ANY)
    dma = pltpu.SemaphoreType.DMA
    peers = seg_size - 1
    far_peers = pts_size - 1
    width = modes // seg_size
    coeffs, gram, proj = pl.pallas_call(
        functools.partial(main_kernel, pts_size, seg_size),
        out_shape=(shape((rank, modes), f32), shape((rank, rank), f32), shape((rank, local), f32)),
        in_specs=[hbm] * 7,
        out_specs=(vmem,) * 3,
        scratch_shapes=[
            pltpu.VMEM((segs, DEPTH), bf16), pltpu.VMEM((segs, DEPTH), bf16),
            pltpu.VMEM((12 * SNAPS, segs), bf16), pltpu.VMEM((3, 128), f32),
            pltpu.VMEM((3, segs), f32), pltpu.VMEM((segs // 128, 128), jnp.int32),
            pltpu.VMEM((1, segs), f32), pltpu.VMEM((1, segs), f32), pltpu.VMEM((1, segs), jnp.int32),
            pltpu.VMEM((3, segs), f32), dma((5,)),
            pltpu.VMEM((3, local), f32),
            pltpu.VMEM((modes, local), f32),
            pltpu.VMEM((peers, 3, local), f32),
            pltpu.VMEM((peers, rank, local), f32),
            pltpu.VMEM((peers, rank, local), f32),
            pltpu.VMEM((12 * SNAPS, local), f32),
            pltpu.VMEM((6 * SNAPS, local), f32),
            pltpu.VMEM((12 * SNAPS, local), f32),
            pltpu.VMEM((6 * SNAPS, local), f32),
            pltpu.VMEM((DEPTH, local), bf16),
            pltpu.VMEM((CHUNK * GROUP, local), bf16),
            pltpu.VMEM((CHUNK * GROUP, local), bf16),
            pltpu.VMEM((seg_size, rank, width), f32),
            pltpu.VMEM((seg_size, rank, width), f32),
            pltpu.VMEM((pts_size, rank, width), f32),
            pltpu.VMEM((2, rank, width), f32),
            pltpu.VMEM((seg_size, rank, width), f32),
            pltpu.VMEM((2, rank, rank), f32),
            pltpu.VMEM((seg_size, rank, rank), f32),
            pltpu.VMEM((pts_size, rank, rank), f32),
            dma((2,)),
            dma((peers,)), dma((peers,)), dma((peers,)), dma((peers,)),
            dma((peers,)), dma((peers,)), dma((far_peers,)), dma((far_peers,)), dma((peers,)), dma((peers,)),
            dma((peers,)), dma((peers,)), dma((far_peers,)), dma((far_peers,)),
        ],
        compiler_params=pltpu.CompilerParams(
            collective_id=0, has_side_effects=True, vmem_limit_bytes=62 * 1024 * 1024),
        name="main",
    )(field_points, wake_nodes, trail_node.reshape(segs // 128, 128), strength[None], core_square[None],
      snapshot[None], stored_modes)
    factor, basis = pl.pallas_call(
        solve_kernel,
        out_shape=(shape((rank, rank), f32), shape((rank, local), f32)),
        in_specs=[vmem] * 2,
        out_specs=(vmem,) * 2,
        compiler_params=pltpu.CompilerParams(vmem_limit_bytes=62 * 1024 * 1024),
        name="solve",
    )(gram, proj)
    return coeffs.T, factor, basis


def solution(mesh):
    return jax.shard_map(
        functools.partial(body, mesh.shape["pts"], mesh.shape["seg"]),
        mesh=mesh,
        in_specs=(
            P(None, ("groups", "pts", "seg")),
            P(None, ("groups", "seg")),
            P(("groups", "seg")),
            P(("groups", "seg")),
            P(("groups", "seg")),
            P(("groups", "seg")),
            P(None, ("groups", "pts", "seg")),
        ),
        out_specs=(P("groups", None), P("groups", None), P(None, ("groups", "pts", "seg"))),
        check_vma=False,
    )
```

```python
import functools
import math

import jax
import jax.numpy as jnp
from jax import lax
from jax.experimental import pallas as pl
from jax.experimental.pallas import tpu as pltpu
from jax.sharding import PartitionSpec as P

SNAPS = 16
HIGH = lax.Precision.HIGHEST
MESH = pl.DeviceIdType.MESH
DEPTH = 32
CHUNK = 256
GROUP = 8
f32 = jnp.float32
bf16 = jnp.bfloat16


def split3(v):
    hi = v.astype(bf16).astype(f32)
    rest = v - hi
    mid = rest.astype(bf16).astype(f32)
    return hi, mid, (rest - mid).astype(bf16).astype(f32)


def left_rows(v):
    hi, mid, lo = split3(v)
    return [hi, hi, mid, hi, lo, mid]


def right_rows(v):
    hi, mid, lo = split3(v)
    return [hi, mid, hi, lo, hi, mid]


def prepare(nodes_in, trail_in, strength_in, core_in, snap_in,
                near_ref, far_ref, weight_ref, centre_ref,
                nodes_ref, trail_ref, strength_ref, core_ref, snap_ref, head_ref, sems):
    pairs = ((nodes_in, nodes_ref), (trail_in, trail_ref), (strength_in, strength_ref),
             (core_in, core_ref), (snap_in, snap_ref))
    copies = [pltpu.make_async_copy(a, b, sems.at[i]) for i, (a, b) in enumerate(pairs)]
    for copy in copies:
        copy.start()
    copies[0].wait()
    copies[1].wait()
    segs = nodes_ref.shape[1]
    rows = segs // 128
    nodes = nodes_ref[...]
    centre = jnp.sum(nodes, axis=1, keepdims=True) * (1.0 / segs)
    centre_ref[...] = jnp.broadcast_to(centre, centre_ref.shape)

    tiles = rows // 8
    high = [trail_ref[8 * r:8 * r + 8, :] // 128 for r in range(tiles)]
    low = [trail_ref[8 * r:8 * r + 8, :] % 128 for r in range(tiles)]

    def look(block, found):
        for at in range(8):
            found = look_row(8 * block + at, found)
        return found

    def look_row(h, found):
        cols = pl.ds(pl.multiple_of(h * 128, 128), 128)
        out = list(found)
        table = [jnp.broadcast_to(nodes_ref[k:k + 1, cols], (8, 128)) for k in range(3)]
        for r in range(tiles):
            here = high[r] == h
            for k in range(3):
                got = jnp.take_along_axis(table[k], low[r], axis=1, mode="promise_in_bounds")
                out[3 * r + k] = jnp.where(here, got, out[3 * r + k])
        return tuple(out)

    found = lax.fori_loop(0, tiles, look, tuple(jnp.zeros((8, 128), f32) for _ in range(3 * tiles)))
    for r in range(tiles):
        for k in range(3):
            for i in range(8):
                at = (8 * r + i) * 128
                head_ref[k:k + 1, at:at + 128] = found[3 * r + k][i:i + 1, :]

    for copy in copies[2:]:
        copy.wait()
    width = 1024
    zero = jnp.zeros((1, width), f32)
    levels = lax.broadcasted_iota(jnp.int32, (SNAPS, width), 0)

    def fill(b, carry):
        cols = pl.ds(pl.multiple_of(b * width, 128), width)
        t = [nodes_ref[k:k + 1, cols] - centre[k:k + 1, :] for k in range(3)]
        h = [head_ref[k:k + 1, cols] - centre[k:k + 1, :] for k in range(3)]
        core = core_ref[:, cols]
        d = [t[k] - h[k] for k in range(3)]
        q = 2.0 * core + (d[0] * d[0] + d[1] * d[1] + d[2] * d[2])
        g = 1.0 / q
        for ref, e in ((near_ref, t), (far_ref, h)):
            square = e[0] * e[0] + e[1] * e[1] + e[2] * e[2] + core
            parts = []
            for k in range(3):
                parts += left_rows(-2.0 * g * e[k])
            parts += left_rows(g) + list(split3(g * square))
            parts += [zero] * (DEPTH - len(parts))
            packed = jnp.concatenate(parts, axis=0)
            ref[pl.ds(pl.multiple_of(b * width, 128), width), :] = packed.T.astype(bf16)
        scale = strength_ref[:, cols] * (2.0 / (4.0 * math.pi)) * g * jnp.sqrt(g)
        v = d + [t[1] * h[2] - t[2] * h[1], t[2] * h[0] - t[0] * h[2], t[0] * h[1] - t[1] * h[0]]
        mine = snap_ref[:, cols] == levels
        for k in range(6):
            value = v[k] * scale
            hi = value.astype(bf16).astype(f32)
            lo = value - hi
            at = SNAPS * k
            weight_ref[at:at + SNAPS, cols] = jnp.where(mine, hi, 0.0).astype(bf16)
            weight_ref[6 * SNAPS + at:6 * SNAPS + at + SNAPS, cols] = jnp.where(mine, lo, 0.0).astype(bf16)
        return carry

    lax.fori_loop(0, segs // width, fill, 0)


def main_kernel(pts_size, seg_size, points_ref, nodes_in, trail_in, strength_in, core_in, snap_in, modes_in,
                coeff_ref, gram_ref, proj_ref,
                near_ref, far_ref, weight_ref, centre_ref,
                nodes_ref, trail_ref, strength_ref, core_ref, snap_ref, head_ref, prep_sems,
                points, modes_ref, peer_points, part_out, part_in, own_both, own_low, both_acc, low_acc,
                side, hi_buf, lo_buf, coeff_part, coeff_seg, coeff_pts, coeff_mine, coeff_all, gram_part, gram_seg, gram_pts,
                local_sem, point_send, point_recv, part_send, part_recv,
                send_a, recv_a, send_b, recv_b, send_c, recv_c, send_d, recv_d, send_e, recv_e):
    group = lax.axis_index("groups")
    pts = lax.axis_index("pts")
    seg = lax.axis_index("seg")
    segs = near_ref.shape[0]
    local = points_ref.shape[1]
    rank = 3 * SNAPS
    width = modes_in.shape[0] // seg_size

    def seg_peer(d):
        return (group, pts, lax.rem(seg + d, seg_size))

    def pts_peer(d):
        return (group, lax.rem(pts + d, pts_size), seg)

    barrier = pltpu.get_barrier_semaphore()
    peers = [seg_peer(d) for d in range(1, seg_size)] + [pts_peer(d) for d in range(1, pts_size)]
    for peer in peers:
        pl.semaphore_signal(barrier, inc=1, device_id=peer, device_id_type=MESH)

    get_points = pltpu.make_async_copy(points_ref, points, local_sem.at[0])
    get_points.start()
    get_modes = pltpu.make_async_copy(modes_in, modes_ref, local_sem.at[1])
    get_modes.start()
    prepare(nodes_in, trail_in, strength_in, core_in, snap_in, near_ref, far_ref, weight_ref, centre_ref,
            nodes_ref, trail_ref, strength_ref, core_ref, snap_ref, head_ref, prep_sems)

    def send(src, dst, send_sem, recv_sem, peer):
        copy = pltpu.make_async_remote_copy(
            src_ref=src, dst_ref=dst, send_sem=send_sem, recv_sem=recv_sem,
            device_id=peer, device_id_type=MESH)
        copy.start()
        return copy

    def place(raw):
        x = [raw[k:k + 1, :] - centre_ref[k:k + 1, 0:1] for k in range(3)]
        rows = []
        for k in range(3):
            rows += right_rows(x[k])
        rows += right_rows(x[0] * x[0] + x[1] * x[1] + x[2] * x[2])
        rows += [jnp.ones((1, local), f32)] * 3
        rows += [jnp.zeros((1, local), f32)] * (DEPTH - len(rows))
        side[...] = jnp.concatenate(rows, axis=0).astype(bf16)
        return x

    def absorb(both, low, first, last):
        def step(i, carry):
            for j in range(GROUP):
                rows = pl.ds(pl.multiple_of(i * (CHUNK * GROUP) + j * CHUNK, CHUNK), CHUNK)
                a2 = jnp.dot(near_ref[rows, :], side[...], preferred_element_type=f32)
                b2 = jnp.dot(far_ref[rows, :], side[...], preferred_element_type=f32)
                ra = lax.rsqrt(a2)
                rb = lax.rsqrt(b2)
                total = a2 * ra + b2 * rb
                factor = (ra + rb) * pl.reciprocal(total * total - 1.0, approx=True)
                hi = factor.astype(bf16)
                hi_buf[j * CHUNK:(j + 1) * CHUNK, :] = hi
                lo_buf[j * CHUNK:(j + 1) * CHUNK, :] = (factor - hi.astype(f32)).astype(bf16)
            cols = pl.ds(pl.multiple_of(i * (CHUNK * GROUP), CHUNK * GROUP), CHUNK * GROUP)
            both[...] += jnp.dot(weight_ref[:, cols], hi_buf[...], preferred_element_type=f32)
            low[...] += jnp.dot(weight_ref[0:6 * SNAPS, cols], lo_buf[...], preferred_element_type=f32)
            return carry

        lax.fori_loop(first, last, step, 0)

    def collect(x, both, low):
        g = both[0:6 * SNAPS, :] + both[6 * SNAPS:12 * SNAPS, :] + low[...]
        g = [g[SNAPS * k:SNAPS * (k + 1), :] for k in range(6)]
        return [
            x[1] * g[2] - x[2] * g[1] + g[3],
            x[2] * g[0] - x[0] * g[2] + g[4],
            x[0] * g[1] - x[1] * g[0] + g[5],
        ]

    steps = segs // (CHUNK * GROUP)
    cut = (steps // 4, steps - steps // 4)
    own_both[...] = jnp.zeros_like(own_both)
    own_low[...] = jnp.zeros_like(own_low)
    get_points.wait()
    place(points[...])
    absorb(own_both, own_low, 0, cut[0])
    pl.semaphore_wait(barrier, len(peers))
    point_copies = [
        send(points, peer_points.at[d - 1], point_send.at[d - 1], point_recv.at[d - 1], seg_peer(d))
        for d in range(1, seg_size)]
    absorb(own_both, own_low, cut[0], cut[1])

    part_copies = []
    for d in range(1, seg_size):
        point_copies[d - 1].wait()
        both_acc[...] = jnp.zeros_like(both_acc)
        low_acc[...] = jnp.zeros_like(low_acc)
        x = place(peer_points[d - 1])
        absorb(both_acc, low_acc, 0, steps)
        for c, block in enumerate(collect(x, both_acc, low_acc)):
            part_out[d - 1, SNAPS * c:SNAPS * (c + 1), :] = block
        part_copies.append(send(
            part_out.at[d - 1], part_in.at[d - 1], part_send.at[d - 1], part_recv.at[d - 1],
            seg_peer(seg_size - d)))
    x = place(points[...])
    absorb(own_both, own_low, cut[1], steps)
    panel = jnp.concatenate(collect(x, own_both, own_low), axis=0)
    for d in range(1, seg_size):
        part_copies[d - 1].wait()
        panel = panel + part_in[d - 1]
    get_modes.wait()

    def spread(src_of, dst, mine, size, peer_of, send_sem, recv_sem):
        copies = [
            send(src_of(d), dst.at[mine], send_sem.at[d - 1], recv_sem.at[d - 1], peer_of(d))
            for d in range(1, size)]
        for copy in copies:
            copy.wait()

    def added(slots, size):
        total = slots[0]
        for i in range(1, size):
            total = total + slots[i]
        return total

    across = (((1,), (1,)), ((), ()))

    def modes_of(q):
        return modes_ref[pl.ds(pl.multiple_of(q * width, width), width), :]

    def product(q):
        return lax.dot_general(panel, modes_of(q), across, precision=HIGH, preferred_element_type=f32)

    copies = []
    for d in range(1, seg_size):
        q = lax.rem(seg + d, seg_size)
        coeff_part[q] = product(q)
        copies.append(send(coeff_part.at[q], coeff_seg.at[seg], send_a.at[d - 1], recv_a.at[d - 1], seg_peer(d)))
    coeff_seg[seg] = product(seg)
    for copy in copies:
        copy.wait()
    coeff_mine[0] = added(coeff_seg, seg_size)
    coeff_pts[pts] = coeff_mine[0]
    spread(lambda d: coeff_mine.at[0], coeff_pts, pts, pts_size, pts_peer, send_b, recv_b)
    coeff_mine[1] = added(coeff_pts, pts_size)
    coeff_all[seg] = coeff_mine[1]
    copies = [
        send(coeff_mine.at[1], coeff_all.at[seg], send_c.at[d - 1], recv_c.at[d - 1], seg_peer(d))
        for d in range(1, seg_size)]
    proj = panel - jnp.dot(coeff_mine[1], modes_of(seg), precision=HIGH, preferred_element_type=f32)
    for d in range(1, seg_size):
        copies[d - 1].wait()
        q = lax.rem(seg + seg_size - d, seg_size)
        proj = proj - jnp.dot(coeff_all[q], modes_of(q), precision=HIGH, preferred_element_type=f32)
    for q in range(seg_size):
        coeff_ref[:, q * width:(q + 1) * width] = coeff_all[q]
    proj_ref[...] = proj
    gram_part[0] = lax.dot_general(proj, proj, across, precision=HIGH, preferred_element_type=f32) * (
        1.0 / (pts_size * seg_size * local))
    gram_seg[seg] = gram_part[0]
    spread(lambda d: gram_part.at[0], gram_seg, seg, seg_size, seg_peer, send_d, recv_d)
    gram_part[1] = added(gram_seg, seg_size)
    gram_pts[pts] = gram_part[1]
    spread(lambda d: gram_part.at[1], gram_pts, pts, pts_size, pts_peer, send_e, recv_e)
    gram_ref[...] = added(gram_pts, pts_size)


def solve_kernel(gram_ref, proj_ref, coeff_ref, factor_ref, basis_ref, coeff_out):
    coeff_out[...] = coeff_ref[...]
    order = gram_ref.shape[0]
    tiles = order // 8
    gram = [gram_ref[8 * t:8 * t + 8, :] for t in range(tiles)]
    right = [proj_ref[8 * t:8 * t + 8, :] for t in range(tiles)]
    row = lax.broadcasted_iota(jnp.int32, (8, 1), 0)
    width = proj_ref.shape[1]
    lanes = min(width, 128)
    for k in range(order):
        at, r = k // 8, k % 8
        cols = [None] * at + [jnp.broadcast_to(gram[t][:, k:k + 1], (8, lanes)) for t in range(at, tiles)]
        pivot = cols[at][r:r + 1, :]
        inv = 1.0 / pivot
        root = lax.rsqrt(pivot)
        line = gram[at][r:r + 1, :]
        side = right[at][r:r + 1, :]
        step = line * inv[:, :order]
        push = side * jnp.concatenate([inv] * (width // lanes), axis=1)
        cols[at] = jnp.where(row > r, cols[at], 0.0)
        for t in range(at, tiles):
            gram[t] = gram[t] - cols[t][:, :order] * step
            right[t] = right[t] - jnp.concatenate([cols[t]] * (width // lanes), axis=1) * push
        gram[at] = jnp.where(row == r, line * root[:, :order], gram[at])
        right[at] = jnp.where(row == r, side * jnp.concatenate([root] * (width // lanes), axis=1), right[at])
    col = lax.broadcasted_iota(jnp.int32, (8, order), 1)
    for t in range(tiles):
        factor_ref[8 * t:8 * t + 8, :] = jnp.where(col >= row + 8 * t, gram[t], 0.0)
        basis_ref[8 * t:8 * t + 8, :] = right[t]


def body(pts_size, seg_size, field_points, wake_nodes, trail_node, strength, core_square, snapshot, stored_modes):
    segs = wake_nodes.shape[1]
    local = field_points.shape[1]
    modes = stored_modes.shape[0]
    rank = 3 * SNAPS
    shape = jax.ShapeDtypeStruct
    vmem = pl.BlockSpec(memory_space=pltpu.VMEM)
    hbm = pl.BlockSpec(memory_space=pl.ANY)
    dma = pltpu.SemaphoreType.DMA
    peers = seg_size - 1
    far_peers = pts_size - 1
    width = modes // seg_size
    coeffs, gram, proj = pl.pallas_call(
        functools.partial(main_kernel, pts_size, seg_size),
        out_shape=(shape((rank, modes), f32), shape((rank, rank), f32), shape((rank, local), f32)),
        in_specs=[hbm] * 7,
        out_specs=(vmem,) * 3,
        scratch_shapes=[
            pltpu.VMEM((segs, DEPTH), bf16), pltpu.VMEM((segs, DEPTH), bf16),
            pltpu.VMEM((12 * SNAPS, segs), bf16), pltpu.VMEM((3, 128), f32),
            pltpu.VMEM((3, segs), f32), pltpu.VMEM((segs // 128, 128), jnp.int32),
            pltpu.VMEM((1, segs), f32), pltpu.VMEM((1, segs), f32), pltpu.VMEM((1, segs), jnp.int32),
            pltpu.VMEM((3, segs), f32), dma((5,)),
            pltpu.VMEM((3, local), f32),
            pltpu.VMEM((modes, local), f32),
            pltpu.VMEM((peers, 3, local), f32),
            pltpu.VMEM((peers, rank, local), f32),
            pltpu.VMEM((peers, rank, local), f32),
            pltpu.VMEM((12 * SNAPS, local), f32),
            pltpu.VMEM((6 * SNAPS, local), f32),
            pltpu.VMEM((12 * SNAPS, local), f32),
            pltpu.VMEM((6 * SNAPS, local), f32),
            pltpu.VMEM((DEPTH, local), bf16),
            pltpu.VMEM((CHUNK * GROUP, local), bf16),
            pltpu.VMEM((CHUNK * GROUP, local), bf16),
            pltpu.VMEM((seg_size, rank, width), f32),
            pltpu.VMEM((seg_size, rank, width), f32),
            pltpu.VMEM((pts_size, rank, width), f32),
            pltpu.VMEM((2, rank, width), f32),
            pltpu.VMEM((seg_size, rank, width), f32),
            pltpu.VMEM((2, rank, rank), f32),
            pltpu.VMEM((seg_size, rank, rank), f32),
            pltpu.VMEM((pts_size, rank, rank), f32),
            dma((2,)),
            dma((peers,)), dma((peers,)), dma((peers,)), dma((peers,)),
            dma((peers,)), dma((peers,)), dma((far_peers,)), dma((far_peers,)), dma((peers,)), dma((peers,)),
            dma((peers,)), dma((peers,)), dma((far_peers,)), dma((far_peers,)),
        ],
        compiler_params=pltpu.CompilerParams(
            collective_id=0, has_side_effects=True, vmem_limit_bytes=62 * 1024 * 1024),
        name="main",
    )(field_points, wake_nodes, trail_node.reshape(segs // 128, 128), strength[None], core_square[None],
      snapshot[None], stored_modes)
    factor, basis, coeffs = pl.pallas_call(
        solve_kernel,
        out_shape=(shape((rank, rank), f32), shape((rank, local), f32), shape((rank, modes), f32)),
        in_specs=[vmem] * 3,
        out_specs=(vmem,) * 3,
        compiler_params=pltpu.CompilerParams(vmem_limit_bytes=62 * 1024 * 1024),
        name="solve",
    )(gram, proj, coeffs)
    return coeffs.T, factor, basis


def solution(mesh):
    return jax.shard_map(
        functools.partial(body, mesh.shape["pts"], mesh.shape["seg"]),
        mesh=mesh,
        in_specs=(
            P(None, ("groups", "pts", "seg")),
            P(None, ("groups", "seg")),
            P(("groups", "seg")),
            P(("groups", "seg")),
            P(("groups", "seg")),
            P(("groups", "seg")),
            P(None, ("groups", "pts", "seg")),
        ),
        out_specs=(P("groups", None), P("groups", None), P(None, ("groups", "pts", "seg"))),
        check_vma=False,
    )
```
